128 devices in a mesh: gx: 16 (over x, y), shot: 8 (over z, core).
Axes of the slice: x: 4, y: 4, z: 4, core: 2. Of those that a mesh axis runs over, the one named last changes fastest.
Arguments:
- wave_prev: float32 [8, 128, 512, 256], P('shot', 'gx'), may hold values from -6 to 6
- wave_now: float32 [8, 128, 512, 256], P('shot', 'gx'), may hold values from -6 to 6
- adjoint_next: float32 [8, 128, 512, 256], P('shot', 'gx'), may hold values from -6 to 6
- adjoint_now: float32 [8, 128, 512, 256], P('shot', 'gx'), may hold values from -6 to 6
- velocity: float32 [128, 512, 256], P('gx'), may hold values from 1.5 to 4.5
- observed: float32 [512, 2, 4096], P('shot', None, 'gx'), may hold values from -0.8 to 0.8
- encode_signs: int32 [8, 512], replicated, may hold values from -1 to 1, as said below
- panel_shot: int32 [512], replicated, may hold values from 0 to 511, each once
- source_position: int32 [3, 512], replicated, may hold values from 0 to 511, as said below
- wavelet: float32 [512, 2], replicated, may hold values from -16 to 16
- receivers: int32 [4096], P('gx'), may hold values from 0 to 1048327, as said below
Outputs:
- wave_next: float32 [8, 128, 512, 256], P('shot', 'gx')
- adjoint_prev: float32 [8, 128, 512, 256], P('shot', 'gx')
- gradient: float32 [128, 512, 256], P('gx', 'shot')
The draws below stay inside these ranges and needn't reach their ends.
Inputs may be any that keep to these rules, and one draw needn't show every extreme that they name: `encode_signs`: each entry is +1 or -1. `panel_shot`: each shot appears in exactly one panel row. `source_position`: row 0 holds x cells below 128, row 1 y cells below 512, row 2 depth cells below 8. `receivers`: entry r is x * 512 * 256 + y * 256 + depth with x below 8, y below 512, depth below 8, a cell of slab r // 256.
All inputs are finite; a program needn't handle non-finite values.
Results may differ from the reference program's by a relative error of at most 0.00023.
Values sent between devices are 32-bit elements; how exact they have to be, the bound alone decides.
A program may use at most 384 MiB of HBM per device.

```python
import math
import jax
import jax.numpy as jnp
from jax import lax

CX = 8
NY = 512
NZ = 256
REC_DEV = 256
NT = 2
NX = 128
SHOTS = 512
SUPERS = 8
RECS = 4096


def draw_encode_signs(key, part):
    return (2 * jax.random.randint(jax.random.fold_in(key, 11), (SUPERS, SHOTS), 0, 2) - 1).astype(jnp.int32)


def draw_source_position(key, part):
    x_key = jax.random.fold_in(key, 21)
    y_key = jax.random.fold_in(key, 22)
    z_key = jax.random.fold_in(key, 23)
    x_cell = jax.random.randint(x_key, (SHOTS,), 0, NX).astype(jnp.int32)
    y_cell = jax.random.randint(y_key, (SHOTS,), 0, NY).astype(jnp.int32)
    z_cell = jax.random.randint(z_key, (SHOTS,), 0, 8).astype(jnp.int32)
    x_cell = x_cell.at[0].set(NX - 1)
    y_cell = y_cell.at[0].set(NY - 1)
    z_cell = z_cell.at[0].set(0)
    return jnp.stack([x_cell, y_cell, z_cell], axis=0).astype(jnp.int32)


def draw_receivers(key, part):
    x_key = jax.random.fold_in(key, 31)
    y_key = jax.random.fold_in(key, 32)
    z_key = jax.random.fold_in(key, 33)
    x_cell = jax.random.randint(x_key, (RECS,), 0, CX)
    y_cell = jax.random.randint(y_key, (RECS,), 0, NY)
    z_cell = jax.random.randint(z_key, (RECS,), 0, 8)
    flat_cell = (x_cell * (NY * NZ) + y_cell * NZ + z_cell).astype(jnp.int32)
    flat_cell = flat_cell.at[0].set((CX - 1) * NY * NZ + (NY - 1) * NZ + 7)
    flat_cell = flat_cell.at[1].set(0)
    return flat_cell.astype(jnp.int32)


def level_of(key, dims, cuts, low, high):
    level = 1.0
    for position, shards_of in cuts:
        draws = jax.random.uniform(jax.random.fold_in(jax.random.fold_in(key, 6), position), (shards_of,), jnp.float32, low / len(cuts), high / len(cuts))
        level = level * jnp.repeat(jnp.exp(draws), dims[position] // shards_of).reshape((-1,) + (1,) * (len(dims) - 1 - position))
    return level


def gaussian(rng, shape, deviation, reach, split=(), kind=jnp.bfloat16):
    result = deviation * jax.random.normal(rng, shape, jnp.float32)
    if split:
        result = result * level_of(rng, shape, split, -0.22, 0.18)
    return jnp.clip(result, -reach, reach).astype(kind)


def setup_inputs(seed: int = 0) -> dict:
    key_of = jax.random.split(jax.random.key(seed), 12)
    return {
        "wave_prev": gaussian(key_of[0], (SUPERS, NX, NY, NZ), 1.0, 6.0, ((0, 8), (1, 16)), jnp.float32),
        "wave_now": gaussian(key_of[1], (SUPERS, NX, NY, NZ), 1.0, 6.0, ((0, 8), (1, 16)), jnp.float32),
        "adjoint_next": gaussian(key_of[2], (SUPERS, NX, NY, NZ), 1.0, 6.0, ((0, 8), (1, 16)), jnp.float32),
        "adjoint_now": gaussian(key_of[3], (SUPERS, NX, NY, NZ), 1.0, 6.0, ((0, 8), (1, 16)), jnp.float32),
        "velocity": jnp.clip(jnp.exp(math.log(4.5) - 1.0986123 * jax.random.uniform(key_of[4], (NX, NY, NZ), jnp.float32) ** level_of(key_of[4], (NX, NY, NZ), ((0, 16),), -0.2, 0.2)), 1.5, 4.5),
        "observed": gaussian(key_of[5], (SHOTS, NT, RECS), 0.1, 0.8, ((0, 8), (2, 16)), jnp.float32),
        "encode_signs": draw_encode_signs(jax.random.fold_in(key_of[11], 71), 0),
        "panel_shot": jax.random.permutation(key_of[7], SHOTS).astype(jnp.int32),
        "source_position": draw_source_position(jax.random.fold_in(key_of[11], 71), 0),
        "wavelet": gaussian(key_of[9], (SHOTS, NT), 4.0, 16.0, (), jnp.float32),
        "receivers": draw_receivers(jax.random.fold_in(key_of[11], 71), 0),
    }


COEFS = (-205.0 / 72.0, 8.0 / 5.0, -1.0 / 5.0, 8.0 / 315.0, -1.0 / 560.0)
STEP_RATIO = 0.09


def stencil(extended):
    x_count = extended.shape[-3] - 8
    inner_part = extended[..., 4:4 + x_count, :, :]
    num_rows = inner_part.shape[-2]
    num_depth = inner_part.shape[-1]
    padding_spec = [(0, 0)] * (inner_part.ndim - 2) + [(4, 4), (4, 4)]
    padded = jnp.pad(inner_part, padding_spec)
    acc_total = (3.0 * COEFS[0]) * inner_part
    for offset in range(1, 5):
        stencil_pair = extended[..., 4 + offset:4 + offset + x_count, :, :] + extended[..., 4 - offset:4 - offset + x_count, :, :]
        stencil_pair = stencil_pair + padded[..., 4 + offset:4 + offset + num_rows, 4:4 + num_depth] + padded[..., 4 - offset:4 - offset + num_rows, 4:4 + num_depth]
        stencil_pair = stencil_pair + padded[..., 4:4 + num_rows, 4 + offset:4 + offset + num_depth] + padded[..., 4:4 + num_rows, 4 - offset:4 - offset + num_depth]
        acc_total = acc_total + COEFS[offset] * stencil_pair
    return acc_total


def reference(wave_prev, wave_now, adjoint_next, adjoint_now, velocity, observed, encode_signs, panel_shot, source_position, wavelet, receivers):
    courant = (velocity * STEP_RATIO) ** 2
    sign_float = encode_signs.astype(jnp.float32)
    sign_panel = sign_float[:, panel_shot]
    encoded = jnp.dot(sign_panel, observed.reshape(SHOTS, NT * RECS), precision=lax.Precision.HIGHEST).reshape(SUPERS, NT, RECS)
    rec_global = (jnp.arange(RECS, dtype=jnp.int32) // REC_DEV) * (CX * NY * NZ) + receivers
    zero_planes = jnp.zeros((4, NY, NZ), jnp.float32)

    def extend(field):
        return jnp.concatenate([zero_planes, field, zero_planes], axis=0)

    def source_field(sign_row, time_index):
        amplitude = sign_row * wavelet[:, time_index]
        return jnp.zeros((NX, NY, NZ), jnp.float32).at[source_position[0], source_position[1], source_position[2]].add(amplitude)

    def inject(resid):
        return jnp.zeros((NX * NY * NZ,), jnp.float32).at[rec_global].add(resid).reshape(NX, NY, NZ)

    def per_super(acc_total, items):
        prev_f, now_f, next_adj, now_adj, sign_row, enc_row = items
        wave_mid = 2.0 * now_f - prev_f + courant * (stencil(extend(now_f)) + source_field(sign_row, 0))
        wave_last = 2.0 * wave_mid - now_f + courant * (stencil(extend(wave_mid)) + source_field(sign_row, 1))
        resid_one = now_f.reshape(-1)[rec_global] - enc_row[0]
        resid_two = wave_mid.reshape(-1)[rec_global] - enc_row[1]
        adjoint_mid = 2.0 * now_adj - next_adj + courant * (stencil(extend(now_adj)) + inject(resid_two))
        adjoint_first = 2.0 * adjoint_mid - now_adj + courant * (stencil(extend(adjoint_mid)) + inject(resid_one))
        image = adjoint_mid * (wave_mid - 2.0 * now_f + prev_f) + now_adj * (wave_last - 2.0 * wave_mid + now_f)
        return acc_total + image, (wave_last, adjoint_first)

    summed, outputs = lax.scan(per_super, jnp.zeros((NX, NY, NZ), jnp.float32), (wave_prev, wave_now, adjoint_next, adjoint_now, sign_float, encoded))
    scale = -2.0 / (velocity * velocity)
    return outputs[0], outputs[1], scale * summed
```

```python
import functools

import jax
import jax.numpy as jnp
from jax import lax
from jax.experimental import pallas as pl
from jax.experimental.pallas import tpu as pltpu
from jax.sharding import PartitionSpec as P

MESH = pl.DeviceIdType.MESH
HIGHEST = lax.Precision.HIGHEST
COEFS = (-205.0 / 72.0, 8.0 / 5.0, -1.0 / 5.0, 8.0 / 315.0, -1.0 / 560.0)
STEP_RATIO = 0.09
PAD = 8
ROWS = 32
LANES = 128
DEEP = 8
S0, S1, NR, D1, D2 = range(5)


def shift_depth(low, high, k, lane):
    if k > 0:
        low_r = pltpu.roll(low, LANES - k, axis=1)
        high_r = pltpu.roll(high, LANES - k, axis=1)
        keep = lane < LANES - k
        return jnp.where(keep, low_r, high_r), jnp.where(keep, high_r, 0.0)
    low_r = pltpu.roll(low, -k, axis=1)
    high_r = pltpu.roll(high, -k, axis=1)
    keep = lane >= -k
    return jnp.where(keep, low_r, 0.0), jnp.where(keep, high_r, low_r)


def kernel(
    n_gx,
    n_shot,
    wp,
    wn,
    ax,
    an,
    vel_hbm,
    obs,
    signs,
    panel,
    srcpos,
    wav,
    recv,
    out_w,
    out_a,
    out_g,
    WN,
    AN,
    WM,
    AM,
    VEL,
    IMG,
    halo,
    stage,
    recv1,
    recv2,
    compact,
    psend,
    precv,
    ograd,
    ssem,
    rsem,
    lsem,
    osem,
    esem,
    ersem,
    s1sem,
    r1sem,
    s2sem,
    r2sem,
):
    cx, ny, nz = VEL.shape
    chunks = ny // ROWS
    share = ny // n_shot
    per_block = share // ROWS
    n_z = n_shot // 2
    g = lax.axis_index("gx")
    s = lax.axis_index("shot")
    z = lax.div(s, 2)
    core = lax.rem(s, 2)
    sibling = s + 1 - 2 * core
    has = (g > 0, g < n_gx - 1)

    barrier = pltpu.get_barrier_semaphore()
    for d in range(2):

        @pl.when(has[d])
        def _():
            pl.semaphore_signal(
                barrier, inc=1, device_id=(g + 2 * d - 1, s), device_id_type=MESH
            )

    for k in range(1, n_shot):
        pl.semaphore_signal(
            barrier, inc=1, device_id=(g, lax.rem(s + k, n_shot)), device_id_type=MESH
        )
    neighbours = has[0].astype(jnp.int32) + has[1].astype(jnp.int32)
    pl.semaphore_wait(barrier, n_shot - 1 + neighbours)

    def rows_of(c, offset=0):
        return pl.ds(pl.multiple_of(c * ROWS + offset, 8), ROWS)

    def halo_copy(h, src, offset, c, d, slot):
        return pltpu.make_async_remote_copy(
            src_ref=src.at[pl.ds(4 * d, 4), rows_of(c, offset), :],
            dst_ref=halo.at[h, slot, :, rows_of(c), :],
            send_sem=ssem.at[h, d, c],
            recv_sem=rsem.at[h, slot, c],
            device_id=(g + 2 * d - 1, s),
            device_id_type=MESH,
        )

    def halo_start(h, src, offset, c):
        for d in range(2):

            @pl.when(has[d])
            def _():
                halo_copy(h, src, offset, c, d, 1 - d).start()

    def halo_wait_recv(h, src, offset, c):
        for d in range(2):

            @pl.when(has[d])
            def _():
                halo_copy(h, src, offset, c, d, d).wait_recv()

    def halo_wait_send(h, src, offset, c):
        for d in range(2):

            @pl.when(has[d])
            def _():
                halo_copy(h, src, offset, c, d, 1 - d).wait_send()

    def loop(n, body):
        def step(i, carry):
            body(i)
            return carry

        lax.fori_loop(0, n, step, 0)

    loop(chunks, lambda c: halo_start(0, wn, 0, c))

    inner = pl.ds(PAD, ny)
    loads = [
        pltpu.make_async_copy(wn, WN.at[:, inner, :], lsem.at[0]),
        pltpu.make_async_copy(vel_hbm, VEL, lsem.at[1]),
        pltpu.make_async_copy(wp, WM.at[:, inner, :], lsem.at[2]),
        pltpu.make_async_copy(an, AN.at[:, inner, :], lsem.at[3]),
        pltpu.make_async_copy(ax, AM.at[:, inner, :], lsem.at[4]),
    ]
    for copy in loads:
        copy.start()
    loop(chunks, lambda c: halo_start(1, an, 0, c))

    n_shots = signs.shape[1]
    sign_float = signs[...].astype(jnp.float32)
    shot_row = lax.broadcasted_iota(jnp.int32, (n_shots, n_shots), 0)
    pick = jnp.where(shot_row == panel[...], 1.0, 0.0)
    sign_panel = jnp.dot(sign_float, pick, preferred_element_type=jnp.float32)
    panels = obs.shape[0]
    sign_panel = pltpu.roll(sign_panel, lax.rem((n_shot - s) * panels, n_shots), axis=1)
    mine = sign_panel[:, :panels]
    n_rec = obs.shape[2]
    for t in range(2):
        part = jnp.dot(
            mine, obs[:, t, :], precision=HIGHEST, preferred_element_type=jnp.float32
        )
        for q in range(n_shot):
            psend[q, :, t * n_rec : (t + 1) * n_rec] = jnp.broadcast_to(
                part[q : q + 1, :], (8, n_rec)
            )

    def panel_copy(k):
        to = lax.rem(s + k, n_shot)
        return pltpu.make_async_remote_copy(
            src_ref=psend.at[to],
            dst_ref=precv.at[k],
            send_sem=esem.at[k],
            recv_sem=ersem.at[k],
            device_id=(g, to),
            device_id_type=MESH,
        )

    for k in range(1, n_shot):
        panel_copy(k).start()

    for field in (WN, AN, WM, AM):
        field[:, 0:PAD, :] = jnp.zeros((cx, PAD, nz), jnp.float32)
        field[:, PAD + ny : 2 * PAD + ny, :] = jnp.zeros((cx, PAD, nz), jnp.float32)
    for d in range(2):

        @pl.when(jnp.logical_not(has[d]))
        def _():
            def clear(i):
                for h in range(4):
                    halo[h, d, :, pl.ds(pl.multiple_of(i * 8, 8), 8), :] = jnp.zeros(
                        (4, 8, nz), jnp.float32
                    )

            loop(ny // 8, clear)

    def one_hot_rows(y):
        return jnp.where(
            lax.broadcasted_iota(jnp.int32, (ny, y.shape[1]), 0) == y, 1.0, 0.0
        )

    def spread(y_hot, values, code):
        slots = lax.broadcasted_iota(jnp.int32, (LANES, code.shape[1]), 0) == code
        return lax.dot_general(
            y_hot,
            jnp.where(slots, values, 0.0),
            (((1,), (1,)), ((), ())),
            precision=HIGHEST,
            preferred_element_type=jnp.float32,
        )

    my_sign = signs[pl.ds(s, 1), :].astype(jnp.float32)
    eye = jnp.where(
        lax.broadcasted_iota(jnp.int32, (8, 2), 0)
        == lax.broadcasted_iota(jnp.int32, (8, 2), 1),
        1.0,
        0.0,
    )
    wave_rows = lax.dot_general(
        eye,
        wav[...],
        (((1,), (1,)), ((), ())),
        precision=HIGHEST,
        preferred_element_type=jnp.float32,
    )
    src_x = srcpos[0:1, :] - g * cx
    inside = (src_x >= 0) & (src_x < cx)
    src_code = jnp.where(inside, src_x * DEEP + srcpos[2:3, :], -1)
    src_hot = one_hot_rows(srcpos[1:2, :])
    compact[S0] = spread(src_hot, my_sign * wave_rows[0:1, :], src_code)
    compact[S1] = spread(src_hot, my_sign * wave_rows[1:2, :], src_code)

    flat = recv[...]
    rec_depth = lax.rem(flat, nz)
    rec_y = lax.rem(lax.div(flat, nz), ny)
    rec_x = lax.div(flat, nz * ny)
    rec_code = rec_x * DEEP + rec_depth
    rec_hot = one_hot_rows(rec_y)
    compact[NR] = spread(rec_hot, jnp.ones((1, n_rec), jnp.float32), rec_code)

    total = psend[s]
    for k in range(1, n_shot):
        panel_copy(k).wait_recv()
        total = total + precv[k]
    compact[D1] = spread(rec_hot, total[0:1, :n_rec], rec_code)
    compact[D2] = spread(rec_hot, total[0:1, n_rec:], rec_code)

    lane = lax.broadcasted_iota(jnp.int32, (8, LANES), 1)
    deep = lane < DEEP

    def laplacian(field, h, x, row):
        def plane(p, half):
            cols = pl.ds(half * LANES, LANES)
            at = pl.ds(pl.multiple_of(row, 8), 8)
            if p < 0:
                return halo[h, 0, p + 4, at, cols]
            if p >= cx:
                return halo[h, 1, p - cx, at, cols]
            return field[p, pl.ds(pl.multiple_of(row + PAD, 8), 8), cols]

        near = pl.ds(pl.multiple_of(row, 8), 8 + 2 * PAD)
        tall = [field[x, near, pl.ds(half * LANES, LANES)] for half in range(2)]

        def moved(k, half):
            return tall[half][PAD + k : PAD + k + 8]

        centre = [plane(x, 0), plane(x, 1)]
        total = [3.0 * COEFS[0] * v for v in centre]
        for k in range(1, 5):
            up = shift_depth(centre[0], centre[1], k, lane)
            down = shift_depth(centre[0], centre[1], -k, lane)
            for half in range(2):
                pair = plane(x + k, half) + plane(x - k, half)
                pair = pair + (moved(k, half) + moved(-k, half))
                pair = pair + (up[half] + down[half])
                total[half] = total[half] + COEFS[k] * pair
        return centre, total

    def compact_at(which, x, row):
        v = compact[which, pl.ds(pl.multiple_of(row, 8), 8), :]
        if x:
            v = pltpu.roll(v, LANES - DEEP * x, axis=1)
        return v

    def courant_at(x, row, half):
        v = VEL[x, pl.ds(pl.multiple_of(row, 8), 8), pl.ds(half * LANES, LANES)]
        v = v * STEP_RATIO
        return v * v

    halves = (pl.ds(0, LANES), pl.ds(LANES, LANES))

    def over_rows(c, body):
        def block(i):
            row = c * ROWS + i * 8
            for x in range(cx):
                body(x, row, i)

        loop(ROWS // 8, block)

    def here(row):
        return pl.ds(pl.multiple_of(row, 8), 8)

    def padded(row):
        return pl.ds(pl.multiple_of(row + PAD, 8), 8)

    for i in (0, 1, 2):
        loads[i].wait()

    def first(x, row, i):
        centre, lap = laplacian(WN, 0, x, row)
        lap[0] = lap[0] + jnp.where(deep, compact_at(S0, x, row), 0.0)
        for half in range(2):
            change = courant_at(x, row, half) * lap[half]
            at = (x, padded(row), halves[half])
            WM[at] = 2.0 * centre[half] - WM[at] + change
            IMG[x, here(row), halves[half]] = change

    def first_chunk(c):
        halo_wait_recv(0, wn, 0, c)
        over_rows(c, first)
        halo_start(2, WM, PAD, c)

    loop(chunks, first_chunk)

    for i in (3, 4):
        loads[i].wait()

    def second(x, row, i):
        centre, lap = laplacian(AN, 1, x, row)
        inject = compact_at(NR, x, row) * WM[x, padded(row), halves[0]] - compact_at(D2, x, row)
        lap[0] = lap[0] + jnp.where(deep, inject, 0.0)
        for half in range(2):
            at = (x, padded(row), halves[half])
            value = 2.0 * centre[half] - AM[at] + courant_at(x, row, half) * lap[half]
            AM[at] = value
            at = (x, here(row), halves[half])
            IMG[at] = IMG[at] * value

    def second_chunk(c):
        halo_wait_recv(1, an, 0, c)
        over_rows(c, second)
        halo_start(3, AM, PAD, c)

    loop(chunks, second_chunk)

    def out_copy(o, out, c):
        slot = lax.rem(c, 2)
        return pltpu.make_async_copy(
            stage.at[o, slot], out.at[:, rows_of(c), :], osem.at[o, slot]
        )

    def pair_copy(j, block):
        return pltpu.make_async_remote_copy(
            src_ref=IMG.at[:, pl.ds(pl.multiple_of(block * share, 8), share), :],
            dst_ref=recv1.at[j],
            send_sem=s1sem.at[j],
            recv_sem=r1sem.at[j],
            device_id=(g, sibling),
            device_id_type=MESH,
        )

    def ring_copy(j, slot):
        return pltpu.make_async_remote_copy(
            src_ref=IMG.at[
                :, pl.ds(pl.multiple_of((2 * j + core) * share, 8), share), :
            ],
            dst_ref=recv2.at[slot],
            send_sem=s2sem.at[j],
            recv_sem=r2sem.at[slot],
            device_id=(g, 2 * j + core),
            device_id_type=MESH,
        )

    def image_share(j):
        pair_copy(j, 2 * j + 1 - core).wait_recv()
        block = 2 * j + core

        def add(i):
            for x in range(cx):
                at = (x, pl.ds(pl.multiple_of(block * share + i * 8, 8), 8), slice(None))
                IMG[at] = IMG[at] + recv1[j, x, pl.ds(pl.multiple_of(i * 8, 8), 8), :]

        loop(share // 8, add)

        @pl.when(j != z)
        def _():
            ring_copy(j, z).start()

    def third(slot):
        def body(x, row, i):
            centre, lap = laplacian(WM, 2, x, row)
            lap[0] = lap[0] + jnp.where(deep, compact_at(S1, x, row), 0.0)
            for half in range(2):
                change = courant_at(x, row, half) * lap[half]
                at = (x, padded(row), halves[half])
                stage[0, slot, x, pl.ds(pl.multiple_of(i * 8, 8), 8), halves[half]] = (
                    2.0 * centre[half] - WN[at] + change
                )
                image = (x, here(row), halves[half])
                IMG[image] = IMG[image] + AN[at] * change

        return body

    def third_chunk(c):
        halo_wait_recv(2, WM, PAD, c)

        @pl.when(c >= 2)
        def _():
            out_copy(0, out_w, c - 2).wait()

        over_rows(c, third(lax.rem(c, 2)))
        out_copy(0, out_w, c).start()

    def third_block(b):
        for i in range(per_block):
            third_chunk(b * per_block + i)

        @pl.when(lax.rem(b, 2) != core)
        def _():
            pair_copy(lax.div(b, 2), b).start()

        @pl.when((lax.rem(b, 2) == 0) & (b >= 2))
        def _():
            image_share(lax.div(b, 2) - 1)

    loop(n_shot, third_block)
    image_share(n_z - 1)

    def fourth(slot):
        def body(x, row, i):
            centre, lap = laplacian(AM, 3, x, row)
            inject = compact_at(NR, x, row) * WN[x, padded(row), halves[0]] - compact_at(D1, x, row)
            lap[0] = lap[0] + jnp.where(deep, inject, 0.0)
            for half in range(2):
                at = (x, padded(row), halves[half])
                stage[1, slot, x, pl.ds(pl.multiple_of(i * 8, 8), 8), halves[half]] = (
                    2.0 * centre[half] - AN[at] + courant_at(x, row, half) * lap[half]
                )

        return body

    def fourth_chunk(c):
        halo_wait_recv(3, AM, PAD, c)

        @pl.when(c >= 2)
        def _():
            out_copy(1, out_a, c - 2).wait()

        over_rows(c, fourth(lax.rem(c, 2)))
        out_copy(1, out_a, c).start()

    def finish_image():
        for k in range(1, n_z):
            ring_copy(lax.rem(z + k, n_z), lax.rem(z + k, n_z)).wait_recv()

        def add(i):
            at8 = pl.ds(pl.multiple_of(i * 8, 8), 8)
            for x in range(cx):
                at = (x, pl.ds(pl.multiple_of(s * share + i * 8, 8), 8), slice(None))
                value = IMG[at]
                for k in range(1, n_z):
                    value = value + recv2[lax.rem(z + k, n_z), x, at8, :]
                v = VEL[at]
                ograd[x, at8, :] = (-2.0 / (v * v)) * value

        loop(share // 8, add)
        pltpu.make_async_copy(ograd, out_g, lsem.at[5]).start()

    def fourth_step(c):
        @pl.when(c == chunks - 2)
        def _():
            finish_image()

        fourth_chunk(c)

    loop(chunks, fourth_step)

    for o, out in ((0, out_w), (1, out_a)):
        for c in (chunks - 2, chunks - 1):
            out_copy(o, out, c).wait()
    pltpu.make_async_copy(ograd, out_g, lsem.at[5]).wait()
    for k in range(1, n_shot):
        panel_copy(k).wait_send()
    for j in range(n_z):
        pair_copy(j, 2 * j + 1 - core).wait_send()

        @pl.when(j != z)
        def _():
            ring_copy(j, z).wait_send()

    def drain(c):
        halo_wait_send(0, wn, 0, c)
        halo_wait_send(1, an, 0, c)
        halo_wait_send(2, WM, PAD, c)
        halo_wait_send(3, AM, PAD, c)

    loop(chunks, drain)


def per_device(n_gx, n_shot, wp, wn, ax, an, velocity, obs, signs, panel, srcpos, wav, recv):
    cx, ny, nz = velocity.shape
    chunks = ny // ROWS
    share = ny // n_shot
    n_z = n_shot // 2
    f32 = jnp.float32
    any_space = pl.BlockSpec(memory_space=pl.ANY)
    vmem = pl.BlockSpec(memory_space=pltpu.VMEM)
    field = (cx, ny + 2 * PAD, nz)
    dma = pltpu.SemaphoreType.DMA
    n_rec = recv.shape[0]
    cells = cx * ny * nz
    out_w, out_a, out_g = pl.pallas_call(
        functools.partial(kernel, n_gx, n_shot),
        out_shape=(
            jax.ShapeDtypeStruct((cx, ny, nz), f32),
            jax.ShapeDtypeStruct((cx, ny, nz), f32),
            jax.ShapeDtypeStruct((cx, share, nz), f32),
        ),
        in_specs=[any_space] * 5 + [vmem] * 6,
        out_specs=(any_space,) * 3,
        scratch_shapes=[
            pltpu.VMEM(field, f32),
            pltpu.VMEM(field, f32),
            pltpu.VMEM(field, f32),
            pltpu.VMEM(field, f32),
            pltpu.VMEM((cx, ny, nz), f32),
            pltpu.VMEM((cx, ny, nz), f32),
            pltpu.VMEM((4, 2, 4, ny, nz), f32),
            pltpu.VMEM((2, 2, cx, ROWS, nz), f32),
            pltpu.VMEM((n_z, cx, share, nz), f32),
            pltpu.VMEM((n_z, cx, share, nz), f32),
            pltpu.VMEM((5, ny, LANES), f32),
            pltpu.VMEM((n_shot, 8, 2 * n_rec), f32),
            pltpu.VMEM((n_shot, 8, 2 * n_rec), f32),
            pltpu.VMEM((cx, share, nz), f32),
            dma((4, 2, chunks)),
            dma((4, 2, chunks)),
            dma((6,)),
            dma((2, 2)),
            dma((n_shot,)),
            dma((n_shot,)),
            dma((n_z,)),
            dma((n_z,)),
            dma((n_z,)),
            dma((n_z,)),
        ],
        compiler_params=pltpu.CompilerParams(
            collective_id=0, has_side_effects=True, vmem_limit_bytes=60 * 2**20
        ),
        cost_estimate=pl.CostEstimate(
            flops=4 * 30 * cells, bytes_accessed=4 * 8 * cells, transcendentals=0
        ),
    )(
        wp.reshape(cx, ny, nz),
        wn.reshape(cx, ny, nz),
        ax.reshape(cx, ny, nz),
        an.reshape(cx, ny, nz),
        velocity,
        obs,
        signs,
        panel.reshape(1, -1),
        srcpos,
        wav,
        recv.reshape(1, -1),
    )
    return out_w[None], out_a[None], out_g


def solution(mesh):
    fields = P("shot", "gx", None, None)
    return jax.shard_map(
        functools.partial(per_device, mesh.shape["gx"], mesh.shape["shot"]),
        mesh=mesh,
        in_specs=(fields,) * 4
        + (P("gx", None, None), P("shot", None, "gx"), P(), P(), P(), P(), P("gx")),
        out_specs=(fields, fields, P("gx", "shot", None)),
        check_vma=False,
    )
```

```python
import functools

import jax
import jax.numpy as jnp
from jax import lax
from jax.experimental import pallas as pl
from jax.experimental.pallas import tpu as pltpu
from jax.sharding import PartitionSpec as P

MESH = pl.DeviceIdType.MESH
HIGHEST = lax.Precision.HIGHEST
COEFS = (-205.0 / 72.0, 8.0 / 5.0, -1.0 / 5.0, 8.0 / 315.0, -1.0 / 560.0)
STEP_RATIO = 0.09
PAD = 8
ROWS = 64
LANES = 128
DEEP = 8
S0, S1, NR, D1, D2 = range(5)


def shift_depth(low, high, k, lane):
    if k > 0:
        low_r = pltpu.roll(low, LANES - k, axis=1)
        high_r = pltpu.roll(high, LANES - k, axis=1)
        keep = lane < LANES - k
        return jnp.where(keep, low_r, high_r), jnp.where(keep, high_r, 0.0)
    low_r = pltpu.roll(low, -k, axis=1)
    high_r = pltpu.roll(high, -k, axis=1)
    keep = lane >= -k
    return jnp.where(keep, low_r, 0.0), jnp.where(keep, high_r, low_r)


def kernel(n_gx, n_shot, *refs):
    (wp, wn, ax, an, vel_hbm), small = refs[:5], refs[5:11]
    out_w, out_a, ograd = refs[11:14]
    WN, AN, WM, AM, VEL, IMG, halo, recv1, recv2, compact, psend, precv = refs[14:26]
    small_vmem = refs[26:32]
    obs, signs, panel, srcpos, wav, recv = small_vmem
    ssem, rsem, lsem, isem, esem, ersem, s1sem, r1sem, s2sem, r2sem, ready = refs[32:]
    cx, ny, nz = VEL.shape
    chunks = ny // ROWS
    share = ny // n_shot
    per_block = share // ROWS
    n_z = n_shot // 2
    g = lax.axis_index("gx")
    s = lax.axis_index("shot")
    z = lax.div(s, 2)
    core = lax.rem(s, 2)
    sibling = s + 1 - 2 * core
    has = (g > 0, g < n_gx - 1)

    rank = 2 * z + 1 - core
    barrier = pltpu.get_barrier_semaphore()
    for d in range(2):

        @pl.when(has[d])
        def _():
            pl.semaphore_signal(
                barrier, inc=1, device_id=(g + 2 * d - 1, s), device_id_type=MESH
            )

    def peer(r):
        return 2 * lax.div(r, 2) + 1 - lax.rem(r, 2)

    for r in range(1, n_shot):

        @pl.when(rank < r)
        def _():
            pl.semaphore_signal(barrier, inc=1, device_id=(g, peer(r)), device_id_type=MESH)

    gathers = [
        pltpu.make_async_copy(source, target, isem.at[i])
        for i, (source, target) in enumerate(zip(small, small_vmem))
    ]
    for copy in gathers:
        copy.start()
    neighbours = has[0].astype(jnp.int32) + has[1].astype(jnp.int32)
    pl.semaphore_wait(barrier, neighbours + rank)

    def rows_of(c, offset=0):
        return pl.ds(pl.multiple_of(c * ROWS + offset, 8), ROWS)

    def halo_copy(h, src, offset, c, d, slot):
        return pltpu.make_async_remote_copy(
            src_ref=src.at[pl.ds(4 * d, 4), rows_of(c, offset), :],
            dst_ref=halo.at[h, slot, :, rows_of(c), :],
            send_sem=ssem.at[h, d, c],
            recv_sem=rsem.at[h, slot, c],
            device_id=(g + 2 * d - 1, s),
            device_id_type=MESH,
        )

    def halo_start(h, src, offset, c):
        for d in range(2):

            @pl.when(has[d])
            def _():
                halo_copy(h, src, offset, c, d, 1 - d).start()

    def halo_wait_recv(h, src, offset, c):
        for d in range(2):

            @pl.when(has[d])
            def _():
                halo_copy(h, src, offset, c, d, d).wait_recv()

    def halo_wait_send(h, src, offset, c):
        for d in range(2):

            @pl.when(has[d])
            def _():
                halo_copy(h, src, offset, c, d, 1 - d).wait_send()

    def loop(n, body):
        def step(i, carry):
            body(i)
            return carry

        lax.fori_loop(0, n, step, 0)

    loop(chunks, lambda c: halo_start(0, wn, 0, c))

    inner = pl.ds(PAD, ny)
    loads = [
        pltpu.make_async_copy(wn, WN.at[:, inner, :], lsem.at[0]),
        pltpu.make_async_copy(vel_hbm, VEL, lsem.at[1]),
        pltpu.make_async_copy(wp, WM.at[:, inner, :], lsem.at[2]),
        pltpu.make_async_copy(an, AN.at[:, inner, :], lsem.at[3]),
        pltpu.make_async_copy(ax, AM.at[:, inner, :], lsem.at[4]),
    ]
    for copy in loads:
        copy.start()
    loop(chunks, lambda c: halo_start(1, an, 0, c))
    for r in range(n_shot - 1):

        @pl.when(rank > r)
        def _():
            pl.semaphore_signal(ready, inc=1, device_id=(g, peer(r)), device_id_type=MESH)


    for copy in gathers:
        copy.wait()
    n_shots = signs.shape[1]
    sign_float = signs[...].astype(jnp.float32)
    shot_row = lax.broadcasted_iota(jnp.int32, (n_shots, n_shots), 0)
    pick = jnp.where(shot_row == panel[...], 1.0, 0.0)
    sign_panel = jnp.dot(sign_float, pick, preferred_element_type=jnp.float32)
    panels = obs.shape[0]
    sign_panel = pltpu.roll(sign_panel, lax.rem((n_shot - s) * panels, n_shots), axis=1)
    mine = sign_panel[:, :panels]
    n_rec = obs.shape[2]
    for t in range(2):
        part = jnp.dot(
            mine, obs[:, t, :], precision=HIGHEST, preferred_element_type=jnp.float32
        )
        for q in range(n_shot):
            psend[q, :, t * n_rec : (t + 1) * n_rec] = jnp.broadcast_to(
                part[q : q + 1, :], (8, n_rec)
            )

    def panel_copy(k):
        to = lax.rem(s + k, n_shot)
        return pltpu.make_async_remote_copy(
            src_ref=psend.at[to],
            dst_ref=precv.at[k],
            send_sem=esem.at[k],
            recv_sem=ersem.at[k],
            device_id=(g, to),
            device_id_type=MESH,
        )


    @pl.when(rank < n_shot - 1)
    def _():
        pl.semaphore_wait(ready, n_shot - 1 - rank)

    for k in range(1, n_shot):
        panel_copy(k).start()

    for field in (WN, AN, WM, AM):
        field[:, 0:PAD, :] = jnp.zeros((cx, PAD, nz), jnp.float32)
        field[:, PAD + ny : 2 * PAD + ny, :] = jnp.zeros((cx, PAD, nz), jnp.float32)
    for d in range(2):

        @pl.when(jnp.logical_not(has[d]))
        def _():
            def clear(i):
                for h in range(4):
                    halo[h, d, :, pl.ds(pl.multiple_of(i * 8, 8), 8), :] = jnp.zeros(
                        (4, 8, nz), jnp.float32
                    )

            loop(ny // 8, clear)

    def one_hot_rows(y):
        return jnp.where(
            lax.broadcasted_iota(jnp.int32, (ny, y.shape[1]), 0) == y, 1.0, 0.0
        )

    def spread(y_hot, values, code):
        slots = lax.broadcasted_iota(jnp.int32, (LANES, code.shape[1]), 0) == code
        return lax.dot_general(
            y_hot,
            jnp.where(slots, values, 0.0),
            (((1,), (1,)), ((), ())),
            precision=HIGHEST,
            preferred_element_type=jnp.float32,
        )

    my_sign = signs[pl.ds(s, 1), :].astype(jnp.float32)
    wave_rows = wav[...]
    src_x = srcpos[0:1, :] - g * cx
    inside = (src_x >= 0) & (src_x < cx)
    src_code = jnp.where(inside, src_x * DEEP + srcpos[2:3, :], -1)
    src_hot = one_hot_rows(srcpos[1:2, :])
    compact[S0] = spread(src_hot, my_sign * wave_rows[0:1, :], src_code)
    compact[S1] = spread(src_hot, my_sign * wave_rows[1:2, :], src_code)

    flat = recv[...]
    rec_depth = lax.rem(flat, nz)
    rec_y = lax.rem(lax.div(flat, nz), ny)
    rec_x = lax.div(flat, nz * ny)
    rec_code = rec_x * DEEP + rec_depth
    rec_hot = one_hot_rows(rec_y)
    compact[NR] = spread(rec_hot, jnp.ones((1, n_rec), jnp.float32), rec_code)

    total = psend[s]
    for k in range(1, n_shot):
        panel_copy(k).wait_recv()
        total = total + precv[k]
    compact[D1] = spread(rec_hot, total[0:1, :n_rec], rec_code)
    compact[D2] = spread(rec_hot, total[0:1, n_rec:], rec_code)

    lane = lax.broadcasted_iota(jnp.int32, (8, LANES), 1)
    deep = lane < DEEP

    def laplacian(field, h, x, row):
        def plane(p, half):
            cols = pl.ds(half * LANES, LANES)
            at = pl.ds(pl.multiple_of(row, 8), 8)
            if p < 0 or p >= cx:
                return 0.0 if h is None else halo[h, int(p >= cx), p % cx % 4, at, cols]
            return field[p, pl.ds(pl.multiple_of(row + PAD, 8), 8), cols]

        near = pl.ds(pl.multiple_of(row, 8), 8 + 2 * PAD)
        tall = [field[x, near, pl.ds(half * LANES, LANES)] for half in range(2)]

        def moved(k, half):
            return tall[half][PAD + k : PAD + k + 8]

        centre = [plane(x, 0), plane(x, 1)]
        total = [3.0 * COEFS[0] * v for v in centre]
        for k in range(1, 5):
            up = shift_depth(centre[0], centre[1], k, lane)
            down = shift_depth(centre[0], centre[1], -k, lane)
            for half in range(2):
                pair = plane(x + k, half) + plane(x - k, half)
                pair = pair + (moved(k, half) + moved(-k, half))
                pair = pair + (up[half] + down[half])
                total[half] = total[half] + COEFS[k] * pair
        return centre, total

    def compact_at(which, x, row):
        v = compact[which, pl.ds(pl.multiple_of(row, 8), 8), :]
        if x:
            v = pltpu.roll(v, LANES - DEEP * x, axis=1)
        return v

    def courant_at(x, row, half):
        v = VEL[x, pl.ds(pl.multiple_of(row, 8), 8), pl.ds(half * LANES, LANES)]
        v = v * STEP_RATIO
        return v * v

    halves = (pl.ds(0, LANES), pl.ds(LANES, LANES))

    def over_rows(c, body):
        def block(i):
            row = c * ROWS + i * 8
            for x in range(cx):
                body(x, row, i)

        loop(ROWS // 8, block)

    def here(row):
        return pl.ds(pl.multiple_of(row, 8), 8)

    def padded(row):
        return pl.ds(pl.multiple_of(row + PAD, 8), 8)

    for i in (0, 1, 2):
        loads[i].wait()

    def first(x, row, i):
        centre, lap = laplacian(WN, 0, x, row)
        lap[0] = lap[0] + jnp.where(deep, compact_at(S0, x, row), 0.0)
        for half in range(2):
            change = courant_at(x, row, half) * lap[half]
            at = (x, padded(row), halves[half])
            WM[at] = 2.0 * centre[half] - WM[at] + change
            IMG[x, here(row), halves[half]] = change

    def first_chunk(c):
        halo_wait_recv(0, wn, 0, c)
        over_rows(c, first)
        halo_start(2, WM, PAD, c)

    loop(chunks, first_chunk)

    for i in (3, 4):
        loads[i].wait()

    def second(x, row, i):
        centre, lap = laplacian(AN, 1, x, row)
        inject = compact_at(NR, x, row) * WM[x, padded(row), halves[0]] - compact_at(D2, x, row)
        lap[0] = lap[0] + jnp.where(deep, inject, 0.0)
        for half in range(2):
            at = (x, padded(row), halves[half])
            value = 2.0 * centre[half] - AM[at] + courant_at(x, row, half) * lap[half]
            AM[at] = value
            at = (x, here(row), halves[half])
            IMG[at] = IMG[at] * value

    def second_chunk(c):
        halo_wait_recv(1, an, 0, c)
        over_rows(c, second)
        halo_start(3, AM, PAD, c)

    loop(chunks, second_chunk)

    def pair_copy(j, block):
        return pltpu.make_async_remote_copy(
            src_ref=IMG.at[:, pl.ds(pl.multiple_of(block * share, 8), share), :],
            dst_ref=recv1.at[j],
            send_sem=s1sem.at[j],
            recv_sem=r1sem.at[j],
            device_id=(g, sibling),
            device_id_type=MESH,
        )

    def ring_copy(j, slot):
        return pltpu.make_async_remote_copy(
            src_ref=IMG.at[
                :, pl.ds(pl.multiple_of((2 * j + core) * share, 8), share), :
            ],
            dst_ref=recv2.at[slot],
            send_sem=s2sem.at[j],
            recv_sem=r2sem.at[slot],
            device_id=(g, 2 * j + core),
            device_id_type=MESH,
        )

    def image_share(j):
        pair_copy(j, 2 * j + 1 - core).wait_recv()
        block = 2 * j + core

        def add(i):
            for x in range(cx):
                at = (x, pl.ds(pl.multiple_of(block * share + i * 8, 8), 8), slice(None))
                IMG[at] = IMG[at] + recv1[j, x, pl.ds(pl.multiple_of(i * 8, 8), 8), :]

        loop(share // 8, add)

        @pl.when(j != z)
        def _():
            ring_copy(j, z).start()

    def third(x, row, i):
        centre, lap = laplacian(WM, 2, x, row)
        lap[0] = lap[0] + jnp.where(deep, compact_at(S1, x, row), 0.0)
        for half in range(2):
            change = courant_at(x, row, half) * lap[half]
            at = (x, padded(row), halves[half])
            image = (x, here(row), halves[half])
            out_w[image] = 2.0 * centre[half] - WN[at] + change
            IMG[image] = IMG[image] + AN[at] * change

    def third_chunk(c):
        halo_wait_recv(2, WM, PAD, c)
        over_rows(c, third)

    def third_block(b):
        for i in range(per_block):
            third_chunk(b * per_block + i)

        @pl.when(lax.rem(b, 2) != core)
        def _():
            pair_copy(lax.div(b, 2), b).start()

        @pl.when((lax.rem(b, 2) == 0) & (b >= 2))
        def _():
            image_share(lax.div(b, 2) - 1)

    loop(n_shot, third_block)
    image_share(n_z - 1)

    def fourth(x, row, i):
        centre, lap = laplacian(AM, None, x, row)
        inject = compact_at(NR, x, row) * WN[x, padded(row), halves[0]] - compact_at(D1, x, row)
        lap[0] = lap[0] + jnp.where(deep, inject, 0.0)
        for half in range(2):
            out_a[x, here(row), halves[half]] = (
                2.0 * centre[half]
                - AN[x, padded(row), halves[half]]
                + courant_at(x, row, half) * lap[half]
            )

    loop(chunks, lambda c: over_rows(c, fourth))

    def fourth_halo(x, row, i):
        side = int(x >= cx // 2)
        for half in range(2):
            more = 0.0
            for k in range(cx - x if side else x + 1, 5):
                p = x + k - cx if side else x - k + 4
                more = more + COEFS[k] * halo[3, side, p, here(row), halves[half]]
            at = (x, here(row), halves[half])
            out_a[at] = out_a[at] + courant_at(x, row, half) * more

    def fourth_chunk(c):
        halo_wait_recv(3, AM, PAD, c)
        over_rows(c, fourth_halo)

    def finish_image():
        for k in range(1, n_z):
            ring_copy(lax.rem(z + k, n_z), lax.rem(z + k, n_z)).wait_recv()

        def add(i):
            at8 = pl.ds(pl.multiple_of(i * 8, 8), 8)
            for x in range(cx):
                at = (x, pl.ds(pl.multiple_of(s * share + i * 8, 8), 8), slice(None))
                value = IMG[at]
                for k in range(1, n_z):
                    value = value + recv2[lax.rem(z + k, n_z), x, at8, :]
                v = VEL[at]
                ograd[x, at8, :] = (-2.0 / (v * v)) * value

        loop(share // 8, add)

    def fourth_step(c):
        @pl.when(c == chunks - 1)
        def _():
            finish_image()

        fourth_chunk(c)

    loop(chunks, fourth_step)

    for k in range(1, n_shot):
        panel_copy(k).wait_send()
    for j in range(n_z):
        pair_copy(j, 2 * j + 1 - core).wait_send()

        @pl.when(j != z)
        def _():
            ring_copy(j, z).wait_send()

    def drain(c):
        halo_wait_send(0, wn, 0, c)
        halo_wait_send(1, an, 0, c)
        halo_wait_send(2, WM, PAD, c)
        halo_wait_send(3, AM, PAD, c)

    loop(chunks, drain)


def copy_out(*refs):
    sems = refs[6]
    copies = [
        pltpu.make_async_copy(refs[i].at[x], refs[3 + i].at[x], sems.at[i, x])
        for i in range(3)
        for x in range(refs[i].shape[0])
    ]
    for copy in copies:
        copy.start()
    for copy in copies:
        copy.wait()


def per_device(n_gx, n_shot, wp, wn, ax, an, velocity, obs, signs, panel, srcpos, wav, recv):
    cx, ny, nz = velocity.shape
    chunks = ny // ROWS
    share = ny // n_shot
    n_z = n_shot // 2
    f32 = jnp.float32
    any_space = pl.BlockSpec(memory_space=pl.ANY)
    vmem = pl.BlockSpec(memory_space=pltpu.VMEM)
    field = (cx, ny + 2 * PAD, nz)
    dma = pltpu.SemaphoreType.DMA
    n_rec = recv.shape[0]
    cells = cx * ny * nz
    small = (obs, signs, panel.reshape(1, -1), srcpos, wav.T, recv.reshape(1, -1))
    shapes = ((cx, ny, nz), (cx, ny, nz), (cx, share, nz))
    results = pl.pallas_call(
        functools.partial(kernel, n_gx, n_shot),
        out_shape=tuple(pltpu.VMEM(shape, f32) for shape in shapes),
        in_specs=[any_space] * 11,
        out_specs=(vmem,) * 3,
        scratch_shapes=[
            pltpu.VMEM(field, f32),
            pltpu.VMEM(field, f32),
            pltpu.VMEM(field, f32),
            pltpu.VMEM(field, f32),
            pltpu.VMEM((cx, ny, nz), f32),
            pltpu.VMEM((cx, ny, nz), f32),
            pltpu.VMEM((4, 2, 4, ny, nz), f32),
            pltpu.VMEM((n_z, cx, share, nz), f32),
            pltpu.VMEM((n_z, cx, share, nz), f32),
            pltpu.VMEM((5, ny, LANES), f32),
            pltpu.VMEM((n_shot, 8, 2 * n_rec), f32),
            pltpu.VMEM((n_shot, 8, 2 * n_rec), f32),
            *(pltpu.VMEM(v.shape, v.dtype) for v in small),
            dma((4, 2, chunks)),
            dma((4, 2, chunks)),
            dma((5,)),
            dma((6,)),
            dma((n_shot,)),
            dma((n_shot,)),
            dma((n_z,)),
            dma((n_z,)),
            dma((n_z,)),
            dma((n_z,)),
            pltpu.SemaphoreType.REGULAR,
        ],
        compiler_params=pltpu.CompilerParams(
            collective_id=0, has_side_effects=True, vmem_limit_bytes=51 * 2**20
        ),
        cost_estimate=pl.CostEstimate(
            flops=4 * 30 * cells, bytes_accessed=4 * 8 * cells, transcendentals=0
        ),
    )(
        wp.reshape(cx, ny, nz),
        wn.reshape(cx, ny, nz),
        ax.reshape(cx, ny, nz),
        an.reshape(cx, ny, nz),
        velocity,
        *small,
    )
    out_w, out_a, out_g = pl.pallas_call(
        copy_out,
        out_shape=tuple(jax.ShapeDtypeStruct(shape, f32) for shape in shapes),
        in_specs=[vmem] * 3,
        out_specs=(any_space,) * 3,
        scratch_shapes=[dma((3, cx))],
        compiler_params=pltpu.CompilerParams(vmem_limit_bytes=2**20),
        cost_estimate=pl.CostEstimate(flops=0, bytes_accessed=8 * 4 * cells, transcendentals=0),
    )(*(pltpu.with_memory_space_constraint(v, pltpu.VMEM) for v in results))
    return out_w[None], out_a[None], out_g


def solution(mesh):
    fields = P("shot", "gx", None, None)
    return jax.shard_map(
        functools.partial(per_device, mesh.shape["gx"], mesh.shape["shot"]),
        mesh=mesh,
        in_specs=(fields,) * 4
        + (P("gx", None, None), P("shot", None, "gx"), P(), P(), P(), P(), P("gx")),
        out_specs=(fields, fields, P("gx", "shot", None)),
        check_vma=False,
    )
```

```python
import functools

import jax
import jax.numpy as jnp
from jax import lax
from jax.experimental import pallas as pl
from jax.experimental.pallas import tpu as pltpu
from jax.sharding import PartitionSpec as P

MESH = pl.DeviceIdType.MESH
HIGHEST = lax.Precision.HIGHEST
COEFS = (-205.0 / 72.0, 8.0 / 5.0, -1.0 / 5.0, 8.0 / 315.0, -1.0 / 560.0)
STEP_RATIO = 0.09
PAD = 8
PARTS = (((0, 8),), ((0, 8),), ((0, 4), (4, 4)), ((0, 7), (7, 1)))
FIRST = (0, 1, 2, 4, 6)
LANES = 128
DEEP = 8
S0, S1, NR, D1, D2 = range(5)


def shift_depth(low, high, k, lane):
    if k > 0:
        low_r = pltpu.roll(low, LANES - k, axis=1)
        high_r = pltpu.roll(high, LANES - k, axis=1)
        keep = lane < LANES - k
        return jnp.where(keep, low_r, high_r), jnp.where(keep, high_r, 0.0)
    low_r = pltpu.roll(low, -k, axis=1)
    high_r = pltpu.roll(high, -k, axis=1)
    keep = lane >= -k
    return jnp.where(keep, low_r, 0.0), jnp.where(keep, high_r, low_r)


def kernel(n_gx, n_shot, *refs):
    (wp, wn, ax, an, vel_hbm), small = refs[:5], refs[5:11]
    out_w, out_a, ograd = refs[11:14]
    WN, AN, WM, AM, VEL, IMG, halo, recv1, recv2, compact, psend, precv = refs[14:26]
    small_vmem = refs[26:32]
    obs, signs, panel, srcpos, wav, recv = small_vmem
    ssem, rsem, isem, esem, ersem, s1sem, r1sem, s2sem, r2sem, ready = refs[32:]
    cx, ny, nz = VEL.shape
    share = ny // n_shot
    n_z = n_shot // 2
    g = lax.axis_index("gx")
    s = lax.axis_index("shot")
    z = lax.div(s, 2)
    core = lax.rem(s, 2)
    sibling = s + 1 - 2 * core
    has = (g > 0, g < n_gx - 1)

    rank = 2 * z + 1 - core
    barrier = pltpu.get_barrier_semaphore()
    for d in range(2):

        @pl.when(has[d])
        def _():
            pl.semaphore_signal(
                barrier, inc=1, device_id=(g + 2 * d - 1, s), device_id_type=MESH
            )

    def peer(r):
        return 2 * lax.div(r, 2) + 1 - lax.rem(r, 2)

    for r in range(1, n_shot):

        @pl.when(rank < r)
        def _():
            pl.semaphore_signal(barrier, inc=1, device_id=(g, peer(r)), device_id_type=MESH)

    gathers = [
        pltpu.make_async_copy(source, target, isem.at[i])
        for i, (source, target) in enumerate(zip(small, small_vmem))
    ]
    for copy in gathers:
        copy.start()
    neighbours = has[0].astype(jnp.int32) + has[1].astype(jnp.int32)
    pl.semaphore_wait(barrier, neighbours + rank)

    def halo_copy(h, i, d, slot):
        unit, count = PARTS[h][i]
        source, first = ((wn, 0), (an, 0), (WM, PAD), (AM, PAD))[h]
        return pltpu.make_async_remote_copy(
            src_ref=source.at[pl.ds(4 * d, 4), pl.ds(first + unit * share, count * share), :],
            dst_ref=halo.at[h, slot, :, pl.ds(unit * share, count * share), :],
            send_sem=ssem.at[d, FIRST[h] + i],
            recv_sem=rsem.at[slot, FIRST[h] + i],
            device_id=(g + 2 * d - 1, s),
            device_id_type=MESH,
        )

    def halo_start(h, i):
        for d in range(2):

            @pl.when(has[d])
            def _():
                halo_copy(h, i, d, 1 - d).start()

    def halo_wait_recv(h, i):
        for d in range(2):

            @pl.when(has[d])
            def _():
                halo_copy(h, i, d, d).wait_recv()

    def halo_wait_send(h, i):
        for d in range(2):

            @pl.when(has[d])
            def _():
                halo_copy(h, i, d, 1 - d).wait_send()

    def start_behind(h, u):
        for i, (unit, count) in enumerate(PARTS[h]):

            @pl.when(u == unit + count - 1)
            def _():
                halo_start(h, i)

    def wait_ahead(h, u):
        for i, (unit, _) in enumerate(PARTS[h]):

            @pl.when(u == unit)
            def _():
                halo_wait_recv(h, i)

    def loop(n, body):
        def step(i, carry):
            body(i)
            return carry

        lax.fori_loop(0, n, step, 0)

    halo_start(0, 0)
    halo_start(1, 0)

    for r in range(n_shot - 1):

        @pl.when(rank > r)
        def _():
            pl.semaphore_signal(ready, inc=1, device_id=(g, peer(r)), device_id_type=MESH)


    for copy in gathers:
        copy.wait()
    inner = pl.ds(PAD, ny)
    loads = [
        pltpu.make_async_copy(wn, WN.at[:, inner, :], isem.at[0]),
        pltpu.make_async_copy(vel_hbm, VEL, isem.at[1]),
        pltpu.make_async_copy(wp, WM.at[:, inner, :], isem.at[2]),
        pltpu.make_async_copy(an, AN.at[:, inner, :], isem.at[3]),
        pltpu.make_async_copy(ax, AM.at[:, inner, :], isem.at[4]),
    ]
    for copy in loads:
        copy.start()
    n_shots = signs.shape[1]
    sign_float = signs[...].astype(jnp.float32)
    shot_row = lax.broadcasted_iota(jnp.int32, (n_shots, n_shots), 0)
    pick = jnp.where(shot_row == panel[...], 1.0, 0.0)
    sign_panel = jnp.dot(sign_float, pick, preferred_element_type=jnp.float32)
    panels = obs.shape[0]
    sign_panel = pltpu.roll(sign_panel, lax.rem((n_shot - s) * panels, n_shots), axis=1)
    mine = sign_panel[:, :panels]
    n_rec = obs.shape[2]
    for t in range(2):
        part = jnp.dot(
            mine, obs[:, t, :], precision=HIGHEST, preferred_element_type=jnp.float32
        )
        for q in range(n_shot):
            psend[q, :, t * n_rec : (t + 1) * n_rec] = jnp.broadcast_to(
                part[q : q + 1, :], (8, n_rec)
            )

    def panel_copy(k):
        to = lax.rem(s + k, n_shot)
        return pltpu.make_async_remote_copy(
            src_ref=psend.at[to],
            dst_ref=precv.at[k - 1],
            send_sem=esem.at[k - 1],
            recv_sem=ersem.at[k - 1],
            device_id=(g, to),
            device_id_type=MESH,
        )


    @pl.when(rank < n_shot - 1)
    def _():
        pl.semaphore_wait(ready, n_shot - 1 - rank)

    for k in range(1, n_shot):
        panel_copy(k).start()

    for field in (WN, AN, WM, AM):
        field[:, 0:PAD, :] = jnp.zeros((cx, PAD, nz), jnp.float32)
        field[:, PAD + ny : 2 * PAD + ny, :] = jnp.zeros((cx, PAD, nz), jnp.float32)
    for d in range(2):

        @pl.when(jnp.logical_not(has[d]))
        def _():
            def clear(i):
                for h in range(4):
                    halo[h, d, :, pl.ds(pl.multiple_of(i * 8, 8), 8), :] = jnp.zeros(
                        (4, 8, nz), jnp.float32
                    )

            loop(ny // 8, clear)

    def one_hot_rows(y):
        return jnp.where(
            lax.broadcasted_iota(jnp.int32, (ny, y.shape[1]), 0) == y, 1.0, 0.0
        )

    def spread(y_hot, values, code):
        slots = lax.broadcasted_iota(jnp.int32, (LANES, code.shape[1]), 0) == code
        return lax.dot_general(
            y_hot,
            jnp.where(slots, values, 0.0),
            (((1,), (1,)), ((), ())),
            precision=HIGHEST,
            preferred_element_type=jnp.float32,
        )

    my_sign = signs[pl.ds(s, 1), :].astype(jnp.float32)
    wave_rows = wav[...]
    src_x = srcpos[0:1, :] - g * cx
    inside = (src_x >= 0) & (src_x < cx)
    src_code = jnp.where(inside, src_x * DEEP + srcpos[2:3, :], -1)
    src_hot = one_hot_rows(srcpos[1:2, :])
    compact[S0] = spread(src_hot, my_sign * wave_rows[0:1, :], src_code)
    compact[S1] = spread(src_hot, my_sign * wave_rows[1:2, :], src_code)

    flat = recv[...]
    rec_depth = lax.rem(flat, nz)
    rec_y = lax.rem(lax.div(flat, nz), ny)
    rec_x = lax.div(flat, nz * ny)
    rec_code = rec_x * DEEP + rec_depth
    rec_hot = one_hot_rows(rec_y)
    compact[NR] = spread(rec_hot, jnp.ones((1, n_rec), jnp.float32), rec_code)

    total = psend[s]
    for k in range(1, n_shot):
        panel_copy(k).wait_recv()
        total = total + precv[k - 1]
    compact[D1] = spread(rec_hot, total[0:1, :n_rec], rec_code)
    compact[D2] = spread(rec_hot, total[0:1, n_rec:], rec_code)

    lane = lax.broadcasted_iota(jnp.int32, (8, LANES), 1)
    deep = lane < DEEP

    def laplacian(field, h, x, row):
        def plane(p, half):
            cols = pl.ds(half * LANES, LANES)
            at = pl.ds(pl.multiple_of(row, 8), 8)
            if p < 0 or p >= cx:
                return 0.0 if h is None else halo[h, int(p >= cx), p % cx % 4, at, cols]
            return field[p, pl.ds(pl.multiple_of(row + PAD, 8), 8), cols]

        near = pl.ds(pl.multiple_of(row, 8), 8 + 2 * PAD)
        tall = [field[x, near, pl.ds(half * LANES, LANES)] for half in range(2)]

        def moved(k, half):
            return tall[half][PAD + k : PAD + k + 8]

        centre = [plane(x, 0), plane(x, 1)]
        total = [3.0 * COEFS[0] * v for v in centre]
        for k in range(1, 5):
            up = shift_depth(centre[0], centre[1], k, lane)
            down = shift_depth(centre[0], centre[1], -k, lane)
            for half in range(2):
                pair = plane(x + k, half) + plane(x - k, half)
                pair = pair + (moved(k, half) + moved(-k, half))
                pair = pair + (up[half] + down[half])
                total[half] = total[half] + COEFS[k] * pair
        return centre, total

    def compact_at(which, x, row):
        v = compact[which, pl.ds(pl.multiple_of(row, 8), 8), :]
        if x:
            v = pltpu.roll(v, LANES - DEEP * x, axis=1)
        return v

    def courant_at(x, row, half):
        v = VEL[x, pl.ds(pl.multiple_of(row, 8), 8), pl.ds(half * LANES, LANES)]
        v = v * STEP_RATIO
        return v * v

    halves = (pl.ds(0, LANES), pl.ds(LANES, LANES))

    def over_rows(c, count, body):
        def block(i):
            row = c * count + i * 8
            for x in range(cx):
                body(x, row)

        loop(count // 8, block)

    def here(row):
        return pl.ds(pl.multiple_of(row, 8), 8)

    def padded(row):
        return pl.ds(pl.multiple_of(row + PAD, 8), 8)

    for i in (0, 1, 2):
        loads[i].wait()

    def first(x, row):
        centre, lap = laplacian(WN, 0, x, row)
        lap[0] = lap[0] + jnp.where(deep, compact_at(S0, x, row), 0.0)
        for half in range(2):
            change = courant_at(x, row, half) * lap[half]
            at = (x, padded(row), halves[half])
            WM[at] = 2.0 * centre[half] - WM[at] + change
            IMG[x, here(row), halves[half]] = change

    def first_unit(u):
        over_rows(u, share, first)
        start_behind(2, u)

    halo_wait_recv(0, 0)
    loop(n_shot, first_unit)

    for i in (3, 4):
        loads[i].wait()

    def second(x, row):
        centre, lap = laplacian(AN, 1, x, row)
        inject = compact_at(NR, x, row) * WM[x, padded(row), halves[0]] - compact_at(D2, x, row)
        lap[0] = lap[0] + jnp.where(deep, inject, 0.0)
        for half in range(2):
            at = (x, padded(row), halves[half])
            value = 2.0 * centre[half] - AM[at] + courant_at(x, row, half) * lap[half]
            AM[at] = value
            at = (x, here(row), halves[half])
            IMG[at] = IMG[at] * value

    def second_unit(u):
        over_rows(u, share, second)
        start_behind(3, u)

    halo_wait_recv(1, 0)
    loop(n_shot, second_unit)

    def pair_copy(j, block):
        return pltpu.make_async_remote_copy(
            src_ref=IMG.at[:, pl.ds(pl.multiple_of(block * share, 8), share), :],
            dst_ref=recv1.at[j],
            send_sem=s1sem.at[j],
            recv_sem=r1sem.at[j],
            device_id=(g, sibling),
            device_id_type=MESH,
        )

    def ring_copy(j, slot):
        return pltpu.make_async_remote_copy(
            src_ref=IMG.at[
                :, pl.ds(pl.multiple_of((2 * j + core) * share, 8), share), :
            ],
            dst_ref=recv2.at[slot],
            send_sem=s2sem.at[j],
            recv_sem=r2sem.at[slot],
            device_id=(g, 2 * j + core),
            device_id_type=MESH,
        )

    def image_share(j):
        pair_copy(j, 2 * j + 1 - core).wait_recv()
        block = 2 * j + core

        def add(i):
            for x in range(cx):
                at = (x, pl.ds(pl.multiple_of(block * share + i * 8, 8), 8), slice(None))
                IMG[at] = IMG[at] + recv1[j, x, pl.ds(pl.multiple_of(i * 8, 8), 8), :]

        loop(share // 8, add)

        @pl.when(j != z)
        def _():
            ring_copy(j, z).start()

    def third(x, row):
        centre, lap = laplacian(WM, 2, x, row)
        lap[0] = lap[0] + jnp.where(deep, compact_at(S1, x, row), 0.0)
        for half in range(2):
            change = courant_at(x, row, half) * lap[half]
            at = (x, padded(row), halves[half])
            image = (x, here(row), halves[half])
            out_w[image] = 2.0 * centre[half] - WN[at] + change
            IMG[image] = IMG[image] + AN[at] * change

    def third_block(b):
        wait_ahead(2, b)
        over_rows(b, share, third)

        @pl.when(lax.rem(b, 2) != core)
        def _():
            pair_copy(lax.div(b, 2), b).start()

        @pl.when((lax.rem(b, 2) == 0) & (b >= 2))
        def _():
            image_share(lax.div(b, 2) - 1)

    loop(n_shot, third_block)
    image_share(n_z - 1)

    def fourth(x, row):
        centre, lap = laplacian(AM, None, x, row)
        inject = compact_at(NR, x, row) * WN[x, padded(row), halves[0]] - compact_at(D1, x, row)
        lap[0] = lap[0] + jnp.where(deep, inject, 0.0)
        for half in range(2):
            out_a[x, here(row), halves[half]] = (
                2.0 * centre[half]
                - AN[x, padded(row), halves[half]]
                + courant_at(x, row, half) * lap[half]
            )

    over_rows(0, ny, fourth)

    def fourth_halo(x, row):
        side = int(x >= cx // 2)
        for half in range(2):
            more = 0.0
            for k in range(cx - x if side else x + 1, 5):
                p = x + k - cx if side else x - k + 4
                more = more + COEFS[k] * halo[3, side, p, here(row), halves[half]]
            at = (x, here(row), halves[half])
            out_a[at] = out_a[at] + courant_at(x, row, half) * more

    def finish_image():
        for k in range(1, n_z):
            ring_copy(lax.rem(z + k, n_z), lax.rem(z + k, n_z)).wait_recv()

        def add(i):
            at8 = pl.ds(pl.multiple_of(i * 8, 8), 8)
            for x in range(cx):
                at = (x, pl.ds(pl.multiple_of(s * share + i * 8, 8), 8), slice(None))
                value = IMG[at]
                for k in range(1, n_z):
                    value = value + recv2[lax.rem(z + k, n_z), x, at8, :]
                v = VEL[at]
                ograd[x, at8, :] = (-2.0 / (v * v)) * value

        loop(share // 8, add)

    last = len(PARTS[3]) - 1
    tail = PARTS[3][last][0]

    def fourth_unit(u):
        wait_ahead(3, u)
        over_rows(u, share, fourth_halo)

    loop(tail, fourth_unit)

    finish_image()
    for k in range(1, n_shot):
        panel_copy(k).wait_send()
    for j in range(n_z):
        pair_copy(j, 2 * j + 1 - core).wait_send()

        @pl.when(j != z)
        def _():
            ring_copy(j, z).wait_send()

    for h in range(4):
        for i in range(len(PARTS[h])):
            if (h, i) != (3, last):
                halo_wait_send(h, i)
    halo_wait_recv(3, last)
    loop(n_shot - tail, lambda u: over_rows(u + tail, share, fourth_halo))
    halo_wait_send(3, last)


def copy_out(*refs):
    sems = refs[6]
    half = refs[0].shape[0] // 2
    parts = [(i, pl.ds(n * half, half)) for i in range(2) for n in range(2)]
    parts.append((2, slice(None)))
    copies = [
        pltpu.make_async_copy(refs[i].at[part], refs[3 + i].at[part], sems.at[n])
        for n, (i, part) in enumerate(parts)
    ]
    for copy in copies:
        copy.start()
    for copy in copies:
        copy.wait()


def per_device(n_gx, n_shot, wp, wn, ax, an, velocity, obs, signs, panel, srcpos, wav, recv):
    cx, ny, nz = velocity.shape
    share = ny // n_shot
    n_z = n_shot // 2
    f32 = jnp.float32
    any_space = pl.BlockSpec(memory_space=pl.ANY)
    vmem = pl.BlockSpec(memory_space=pltpu.VMEM)
    field = (cx, ny + 2 * PAD, nz)
    dma = pltpu.SemaphoreType.DMA
    n_rec = recv.shape[0]
    cells = cx * ny * nz
    small = (obs, signs, panel.reshape(1, -1), srcpos, wav.T, recv.reshape(1, -1))
    shapes = ((cx, ny, nz), (cx, ny, nz), (cx, share, nz))
    results = pl.pallas_call(
        functools.partial(kernel, n_gx, n_shot),
        out_shape=tuple(pltpu.VMEM(shape, f32) for shape in shapes),
        in_specs=[any_space] * 11,
        out_specs=(vmem,) * 3,
        scratch_shapes=[
            pltpu.VMEM(field, f32),
            pltpu.VMEM(field, f32),
            pltpu.VMEM(field, f32),
            pltpu.VMEM(field, f32),
            pltpu.VMEM((cx, ny, nz), f32),
            pltpu.VMEM((cx, ny, nz), f32),
            pltpu.VMEM((4, 2, 4, ny, nz), f32),
            pltpu.VMEM((n_z, cx, share, nz), f32),
            pltpu.VMEM((n_z, cx, share, nz), f32),
            pltpu.VMEM((5, ny, LANES), f32),
            pltpu.VMEM((n_shot, 8, 2 * n_rec), f32),
            pltpu.VMEM((n_shot - 1, 8, 2 * n_rec), f32),
            *(pltpu.VMEM(v.shape, v.dtype) for v in small),
            dma((2, FIRST[4])),
            dma((2, FIRST[4])),
            dma((6,)),
            dma((n_shot - 1,)),
            dma((n_shot - 1,)),
            dma((n_z,)),
            dma((n_z,)),
            dma((n_z,)),
            dma((n_z,)),
            pltpu.SemaphoreType.REGULAR,
        ],
        compiler_params=pltpu.CompilerParams(
            collective_id=0, has_side_effects=True, vmem_limit_bytes=51 * 2**20
        ),
        cost_estimate=pl.CostEstimate(
            flops=4 * 30 * cells, bytes_accessed=4 * 8 * cells, transcendentals=0
        ),
    )(
        wp.reshape(cx, ny, nz),
        wn.reshape(cx, ny, nz),
        ax.reshape(cx, ny, nz),
        an.reshape(cx, ny, nz),
        velocity,
        *small,
    )
    out_w, out_a, out_g = pl.pallas_call(
        copy_out,
        out_shape=tuple(jax.ShapeDtypeStruct(shape, f32) for shape in shapes),
        in_specs=[vmem] * 3,
        out_specs=(any_space,) * 3,
        scratch_shapes=[dma((5,))],
        compiler_params=pltpu.CompilerParams(vmem_limit_bytes=2**20),
        cost_estimate=pl.CostEstimate(flops=0, bytes_accessed=8 * 4 * cells, transcendentals=0),
    )(*(pltpu.with_memory_space_constraint(v, pltpu.VMEM) for v in results))
    return out_w[None], out_a[None], out_g


def solution(mesh):
    fields = P("shot", "gx", None, None)
    return jax.shard_map(
        functools.partial(per_device, mesh.shape["gx"], mesh.shape["shot"]),
        mesh=mesh,
        in_specs=(fields,) * 4
        + (P("gx", None, None), P("shot", None, "gx"), P(), P(), P(), P(), P("gx")),
        out_specs=(fields, fields, P("gx", "shot", None)),
        check_vma=False,
    )
```

```python
import functools

import jax
import jax.numpy as jnp
from jax import lax
from jax.experimental import pallas as pl
from jax.experimental.pallas import tpu as pltpu
from jax.sharding import PartitionSpec as P

MESH = pl.DeviceIdType.MESH
HIGHEST = lax.Precision.HIGHEST
COEFS = (-205.0 / 72.0, 8.0 / 5.0, -1.0 / 5.0, 8.0 / 315.0, -1.0 / 560.0)
STEP_RATIO = 0.09
PAD = 8
PARTS = (((0, 8),), ((0, 8),), ((0, 4), (4, 4)), ((0, 7), (7, 1)))
FIRST = (0, 1, 2, 4, 6)
LANES = 128
DEEP = 8
S0, S1, NR, D1, D2 = range(5)


def shift_depth(low, high, k, lane):
    if k > 0:
        low_r = pltpu.roll(low, LANES - k, axis=1)
        high_r = pltpu.roll(high, LANES - k, axis=1)
        keep = lane < LANES - k
        return jnp.where(keep, low_r, high_r), jnp.where(keep, high_r, 0.0)
    low_r = pltpu.roll(low, -k, axis=1)
    high_r = pltpu.roll(high, -k, axis=1)
    keep = lane >= -k
    return jnp.where(keep, low_r, 0.0), jnp.where(keep, high_r, low_r)


def kernel(n_gx, n_shot, *refs):
    (wp, wn, ax, an, vel_hbm), small = refs[:5], refs[5:11]
    out_w, out_a, ograd = refs[11:14]
    WN, AN, WM, AM, VEL, IMG, halo, recv1, recv2, compact, psend, ppair, psum, precv = refs[14:28]
    small_vmem = refs[28:34]
    obs, signs, panel, srcpos, wav, recv = small_vmem
    ssem, rsem, isem, esem, ersem, s1sem, r1sem, s2sem, r2sem, ready = refs[34:]
    cx, ny, nz = VEL.shape
    share = ny // n_shot
    n_z = n_shot // 2
    g = lax.axis_index("gx")
    s = lax.axis_index("shot")
    z = lax.div(s, 2)
    core = lax.rem(s, 2)
    sibling = s + 1 - 2 * core
    has = (g > 0, g < n_gx - 1)

    barrier = pltpu.get_barrier_semaphore()
    for d in range(2):

        @pl.when(has[d])
        def _():
            pl.semaphore_signal(
                barrier, inc=1, device_id=(g + 2 * d - 1, s), device_id_type=MESH
            )

    @pl.when(core == 1)
    def _():
        pl.semaphore_signal(barrier, inc=1, device_id=(g, sibling), device_id_type=MESH)

    for q in range(1, n_z):

        @pl.when(z < q)
        def _():
            pl.semaphore_signal(barrier, inc=1, device_id=(g, 2 * q + core), device_id_type=MESH)

    gathers = [
        pltpu.make_async_copy(source, target, isem.at[i])
        for i, (source, target) in enumerate(zip(small, small_vmem))
    ]
    for copy in gathers:
        copy.start()
    neighbours = has[0].astype(jnp.int32) + has[1].astype(jnp.int32)
    pl.semaphore_wait(barrier, neighbours + z + 1 - core)

    def halo_copy(h, i, d, slot):
        unit, count = PARTS[h][i]
        source, first = ((wn, 0), (an, 0), (WM, PAD), (AM, PAD))[h]
        return pltpu.make_async_remote_copy(
            src_ref=source.at[pl.ds(4 * d, 4), pl.ds(first + unit * share, count * share), :],
            dst_ref=halo.at[h, slot, :, pl.ds(unit * share, count * share), :],
            send_sem=ssem.at[d, FIRST[h] + i],
            recv_sem=rsem.at[slot, FIRST[h] + i],
            device_id=(g + 2 * d - 1, s),
            device_id_type=MESH,
        )

    def halo_start(h, i):
        for d in range(2):

            @pl.when(has[d])
            def _():
                halo_copy(h, i, d, 1 - d).start()

    def halo_wait_recv(h, i):
        for d in range(2):

            @pl.when(has[d])
            def _():
                halo_copy(h, i, d, d).wait_recv()

    def halo_wait_send(h, i):
        for d in range(2):

            @pl.when(has[d])
            def _():
                halo_copy(h, i, d, 1 - d).wait_send()

    def start_behind(h, u):
        for i, (unit, count) in enumerate(PARTS[h]):

            @pl.when(u == unit + count - 1)
            def _():
                halo_start(h, i)

    def wait_ahead(h, u):
        for i, (unit, _) in enumerate(PARTS[h]):

            @pl.when(u == unit)
            def _():
                halo_wait_recv(h, i)

    def loop(n, body):
        def step(i, carry):
            body(i)
            return carry

        lax.fori_loop(0, n, step, 0)

    halo_start(0, 0)
    halo_start(1, 0)

    @pl.when(core == 0)
    def _():
        pl.semaphore_signal(ready, inc=1, device_id=(g, sibling), device_id_type=MESH)

    for q in range(n_z - 1):

        @pl.when(z > q)
        def _():
            pl.semaphore_signal(ready, inc=1, device_id=(g, 2 * q + core), device_id_type=MESH)

    for copy in gathers:
        copy.wait()
    inner = pl.ds(PAD, ny)
    loads = [
        pltpu.make_async_copy(wn, WN.at[:, inner, :], isem.at[0]),
        pltpu.make_async_copy(vel_hbm, VEL, isem.at[1]),
        pltpu.make_async_copy(wp, WM.at[:, inner, :], isem.at[2]),
        pltpu.make_async_copy(an, AN.at[:, inner, :], isem.at[3]),
        pltpu.make_async_copy(ax, AM.at[:, inner, :], isem.at[4]),
    ]
    for copy in loads:
        copy.start()
    n_shots = signs.shape[1]
    sign_float = signs[...].astype(jnp.float32)
    shot_row = lax.broadcasted_iota(jnp.int32, (n_shots, n_shots), 0)
    pick = jnp.where(shot_row == panel[...], 1.0, 0.0)
    sign_panel = jnp.dot(sign_float, pick, preferred_element_type=jnp.float32)
    panels = obs.shape[0]
    sign_panel = pltpu.roll(sign_panel, lax.rem((n_shot - s) * panels, n_shots), axis=1)
    mine = sign_panel[:, :panels]
    n_rec = obs.shape[2]
    for t in range(2):
        part = jnp.dot(
            mine, obs[:, t, :], precision=HIGHEST, preferred_element_type=jnp.float32
        )
        for q in range(n_shot):
            psend[q % 2, q // 2, :, t * n_rec : (t + 1) * n_rec] = jnp.broadcast_to(
                part[q : q + 1, :], (8, n_rec)
            )

    def panel_pair():
        return pltpu.make_async_remote_copy(
            src_ref=psend.at[1 - core],
            dst_ref=ppair,
            send_sem=esem.at[0],
            recv_sem=ersem.at[0],
            device_id=(g, sibling),
            device_id_type=MESH,
        )

    def panel_copy(k):
        to = lax.rem(z + k, n_z)
        return pltpu.make_async_remote_copy(
            src_ref=psum.at[to],
            dst_ref=precv.at[k - 1],
            send_sem=esem.at[k],
            recv_sem=ersem.at[k],
            device_id=(g, 2 * to + core),
            device_id_type=MESH,
        )

    answers = n_z - 1 - z + core

    @pl.when(answers > 0)
    def _():
        pl.semaphore_wait(ready, answers)

    panel_pair().start()

    for field in (WN, AN, WM, AM):
        field[:, 0:PAD, :] = jnp.zeros((cx, PAD, nz), jnp.float32)
        field[:, PAD + ny : 2 * PAD + ny, :] = jnp.zeros((cx, PAD, nz), jnp.float32)
    for d in range(2):

        @pl.when(jnp.logical_not(has[d]))
        def _():
            def clear(i):
                for h in range(4):
                    halo[h, d, :, pl.ds(pl.multiple_of(i * 8, 8), 8), :] = jnp.zeros(
                        (4, 8, nz), jnp.float32
                    )

            loop(ny // 8, clear)

    panel_pair().wait_recv()
    psum[...] = psend[core] + ppair[...]
    for k in range(1, n_z):
        panel_copy(k).start()

    def one_hot_rows(y):
        return jnp.where(
            lax.broadcasted_iota(jnp.int32, (ny, y.shape[1]), 0) == y, 1.0, 0.0
        )

    def spread(y_hot, values, code):
        slots = lax.broadcasted_iota(jnp.int32, (LANES, code.shape[1]), 0) == code
        return lax.dot_general(
            y_hot,
            jnp.where(slots, values, 0.0),
            (((1,), (1,)), ((), ())),
            precision=HIGHEST,
            preferred_element_type=jnp.float32,
        )

    my_sign = signs[pl.ds(s, 1), :].astype(jnp.float32)
    wave_rows = wav[...]
    src_x = srcpos[0:1, :] - g * cx
    inside = (src_x >= 0) & (src_x < cx)
    src_code = jnp.where(inside, src_x * DEEP + srcpos[2:3, :], -1)
    src_hot = one_hot_rows(srcpos[1:2, :])
    compact[S0] = spread(src_hot, my_sign * wave_rows[0:1, :], src_code)
    compact[S1] = spread(src_hot, my_sign * wave_rows[1:2, :], src_code)

    flat = recv[...]
    rec_depth = lax.rem(flat, nz)
    rec_y = lax.rem(lax.div(flat, nz), ny)
    rec_x = lax.div(flat, nz * ny)
    rec_code = rec_x * DEEP + rec_depth
    rec_hot = one_hot_rows(rec_y)
    compact[NR] = spread(rec_hot, jnp.ones((1, n_rec), jnp.float32), rec_code)

    total = psum[z]
    for k in range(1, n_z):
        panel_copy(k).wait_recv()
        total = total + precv[k - 1]
    compact[D1] = spread(rec_hot, total[0:1, :n_rec], rec_code)
    compact[D2] = spread(rec_hot, total[0:1, n_rec:], rec_code)

    lane = lax.broadcasted_iota(jnp.int32, (8, LANES), 1)
    deep = lane < DEEP

    def laplacian(field, h, x, row):
        def plane(p, half):
            cols = pl.ds(half * LANES, LANES)
            at = pl.ds(pl.multiple_of(row, 8), 8)
            if p < 0 or p >= cx:
                return 0.0 if h is None else halo[h, int(p >= cx), p % cx % 4, at, cols]
            return field[p, pl.ds(pl.multiple_of(row + PAD, 8), 8), cols]

        near = pl.ds(pl.multiple_of(row, 8), 8 + 2 * PAD)
        tall = [field[x, near, pl.ds(half * LANES, LANES)] for half in range(2)]

        def moved(k, half):
            return tall[half][PAD + k : PAD + k + 8]

        centre = [plane(x, 0), plane(x, 1)]
        total = [3.0 * COEFS[0] * v for v in centre]
        for k in range(1, 5):
            up = shift_depth(centre[0], centre[1], k, lane)
            down = shift_depth(centre[0], centre[1], -k, lane)
            for half in range(2):
                pair = plane(x + k, half) + plane(x - k, half)
                pair = pair + (moved(k, half) + moved(-k, half))
                pair = pair + (up[half] + down[half])
                total[half] = total[half] + COEFS[k] * pair
        return centre, total

    def compact_at(which, x, row):
        v = compact[which, pl.ds(pl.multiple_of(row, 8), 8), :]
        if x:
            v = pltpu.roll(v, LANES - DEEP * x, axis=1)
        return v

    def courant_at(x, row, half):
        v = VEL[x, pl.ds(pl.multiple_of(row, 8), 8), pl.ds(half * LANES, LANES)]
        v = v * STEP_RATIO
        return v * v

    halves = (pl.ds(0, LANES), pl.ds(LANES, LANES))

    def over_rows(c, count, body):
        def block(i):
            row = c * count + i * 8
            for x in range(cx):
                body(x, row)

        loop(count // 8, block)

    def here(row):
        return pl.ds(pl.multiple_of(row, 8), 8)

    def padded(row):
        return pl.ds(pl.multiple_of(row + PAD, 8), 8)

    for i in (0, 1, 2):
        loads[i].wait()

    def first(x, row):
        centre, lap = laplacian(WN, 0, x, row)
        lap[0] = lap[0] + jnp.where(deep, compact_at(S0, x, row), 0.0)
        for half in range(2):
            change = courant_at(x, row, half) * lap[half]
            at = (x, padded(row), halves[half])
            WM[at] = 2.0 * centre[half] - WM[at] + change
            IMG[x, here(row), halves[half]] = change

    def first_unit(u):
        over_rows(u, share, first)
        start_behind(2, u)

    halo_wait_recv(0, 0)
    loop(n_shot, first_unit)

    for i in (3, 4):
        loads[i].wait()

    def second(x, row):
        centre, lap = laplacian(AN, 1, x, row)
        inject = compact_at(NR, x, row) * WM[x, padded(row), halves[0]] - compact_at(D2, x, row)
        lap[0] = lap[0] + jnp.where(deep, inject, 0.0)
        for half in range(2):
            at = (x, padded(row), halves[half])
            value = 2.0 * centre[half] - AM[at] + courant_at(x, row, half) * lap[half]
            AM[at] = value
            at = (x, here(row), halves[half])
            IMG[at] = IMG[at] * value

    def second_unit(u):
        over_rows(u, share, second)
        start_behind(3, u)

    halo_wait_recv(1, 0)
    loop(n_shot, second_unit)

    def pair_copy(j, block):
        return pltpu.make_async_remote_copy(
            src_ref=IMG.at[:, pl.ds(pl.multiple_of(block * share, 8), share), :],
            dst_ref=recv1.at[j],
            send_sem=s1sem.at[j],
            recv_sem=r1sem.at[j],
            device_id=(g, sibling),
            device_id_type=MESH,
        )

    def ring_copy(j, slot):
        return pltpu.make_async_remote_copy(
            src_ref=IMG.at[
                :, pl.ds(pl.multiple_of((2 * j + core) * share, 8), share), :
            ],
            dst_ref=recv2.at[slot],
            send_sem=s2sem.at[j],
            recv_sem=r2sem.at[slot],
            device_id=(g, 2 * j + core),
            device_id_type=MESH,
        )

    def image_share(j):
        pair_copy(j, 2 * j + 1 - core).wait_recv()
        block = 2 * j + core

        def add(i):
            for x in range(cx):
                at = (x, pl.ds(pl.multiple_of(block * share + i * 8, 8), 8), slice(None))
                IMG[at] = IMG[at] + recv1[j, x, pl.ds(pl.multiple_of(i * 8, 8), 8), :]

        loop(share // 8, add)

        @pl.when(j != z)
        def _():
            ring_copy(j, z).start()

    def third(x, row):
        centre, lap = laplacian(WM, 2, x, row)
        lap[0] = lap[0] + jnp.where(deep, compact_at(S1, x, row), 0.0)
        for half in range(2):
            change = courant_at(x, row, half) * lap[half]
            at = (x, padded(row), halves[half])
            image = (x, here(row), halves[half])
            out_w[image] = 2.0 * centre[half] - WN[at] + change
            IMG[image] = IMG[image] + AN[at] * change

    def third_block(b):
        wait_ahead(2, b)
        over_rows(b, share, third)

        @pl.when(lax.rem(b, 2) != core)
        def _():
            pair_copy(lax.div(b, 2), b).start()

        @pl.when((lax.rem(b, 2) == 0) & (b >= 2))
        def _():
            image_share(lax.div(b, 2) - 1)

    loop(n_shot, third_block)
    image_share(n_z - 1)

    def fourth(x, row):
        centre, lap = laplacian(AM, None, x, row)
        inject = compact_at(NR, x, row) * WN[x, padded(row), halves[0]] - compact_at(D1, x, row)
        lap[0] = lap[0] + jnp.where(deep, inject, 0.0)
        for half in range(2):
            out_a[x, here(row), halves[half]] = (
                2.0 * centre[half]
                - AN[x, padded(row), halves[half]]
                + courant_at(x, row, half) * lap[half]
            )

    over_rows(0, ny, fourth)

    def fourth_halo(x, row):
        side = int(x >= cx // 2)
        for half in range(2):
            more = 0.0
            for k in range(cx - x if side else x + 1, 5):
                p = x + k - cx if side else x - k + 4
                more = more + COEFS[k] * halo[3, side, p, here(row), halves[half]]
            at = (x, here(row), halves[half])
            out_a[at] = out_a[at] + courant_at(x, row, half) * more

    def finish_image():
        for k in range(1, n_z):
            ring_copy(lax.rem(z + k, n_z), lax.rem(z + k, n_z)).wait_recv()

        def add(i):
            at8 = pl.ds(pl.multiple_of(i * 8, 8), 8)
            for x in range(cx):
                at = (x, pl.ds(pl.multiple_of(s * share + i * 8, 8), 8), slice(None))
                value = IMG[at]
                for k in range(1, n_z):
                    value = value + recv2[lax.rem(z + k, n_z), x, at8, :]
                v = VEL[at]
                ograd[x, at8, :] = (-2.0 / (v * v)) * value

        loop(share // 8, add)

    last = len(PARTS[3]) - 1
    tail = PARTS[3][last][0]

    def fourth_unit(u):
        wait_ahead(3, u)
        over_rows(u, share, fourth_halo)

    loop(tail, fourth_unit)

    finish_image()
    panel_pair().wait_send()
    for k in range(1, n_z):
        panel_copy(k).wait_send()
    for j in range(n_z):
        pair_copy(j, 2 * j + 1 - core).wait_send()

        @pl.when(j != z)
        def _():
            ring_copy(j, z).wait_send()

    for h in range(4):
        for i in range(len(PARTS[h])):
            if (h, i) != (3, last):
                halo_wait_send(h, i)
    halo_wait_recv(3, last)
    loop(n_shot - tail, lambda u: over_rows(u + tail, share, fourth_halo))
    halo_wait_send(3, last)


def copy_out(*refs):
    sems = refs[6]
    half = refs[0].shape[0] // 2
    parts = [(i, pl.ds(n * half, half)) for i in range(2) for n in range(2)]
    parts.append((2, slice(None)))
    copies = [
        pltpu.make_async_copy(refs[i].at[part], refs[3 + i].at[part], sems.at[n])
        for n, (i, part) in enumerate(parts)
    ]
    for copy in copies:
        copy.start()
    for copy in copies:
        copy.wait()


def per_device(n_gx, n_shot, wp, wn, ax, an, velocity, obs, signs, panel, srcpos, wav, recv):
    cx, ny, nz = velocity.shape
    share = ny // n_shot
    n_z = n_shot // 2
    f32 = jnp.float32
    any_space = pl.BlockSpec(memory_space=pl.ANY)
    vmem = pl.BlockSpec(memory_space=pltpu.VMEM)
    field = (cx, ny + 2 * PAD, nz)
    dma = pltpu.SemaphoreType.DMA
    n_rec = recv.shape[0]
    cells = cx * ny * nz
    small = (obs, signs, panel.reshape(1, -1), srcpos, wav.T, recv.reshape(1, -1))
    shapes = ((cx, ny, nz), (cx, ny, nz), (cx, share, nz))
    results = pl.pallas_call(
        functools.partial(kernel, n_gx, n_shot),
        out_shape=tuple(pltpu.VMEM(shape, f32) for shape in shapes),
        in_specs=[any_space] * 11,
        out_specs=(vmem,) * 3,
        scratch_shapes=[
            pltpu.VMEM(field, f32),
            pltpu.VMEM(field, f32),
            pltpu.VMEM(field, f32),
            pltpu.VMEM(field, f32),
            pltpu.VMEM((cx, ny, nz), f32),
            pltpu.VMEM((cx, ny, nz), f32),
            pltpu.VMEM((4, 2, 4, ny, nz), f32),
            pltpu.VMEM((n_z, cx, share, nz), f32),
            pltpu.VMEM((n_z, cx, share, nz), f32),
            pltpu.VMEM((5, ny, LANES), f32),
            pltpu.VMEM((2, n_z, 8, 2 * n_rec), f32),
            pltpu.VMEM((n_z, 8, 2 * n_rec), f32),
            pltpu.VMEM((n_z, 8, 2 * n_rec), f32),
            pltpu.VMEM((n_z - 1, 8, 2 * n_rec), f32),
            *(pltpu.VMEM(v.shape, v.dtype) for v in small),
            dma((2, FIRST[4])),
            dma((2, FIRST[4])),
            dma((6,)),
            dma((n_z,)),
            dma((n_z,)),
            dma((n_z,)),
            dma((n_z,)),
            dma((n_z,)),
            dma((n_z,)),
            pltpu.SemaphoreType.REGULAR,
        ],
        compiler_params=pltpu.CompilerParams(
            collective_id=0, has_side_effects=True, vmem_limit_bytes=51 * 2**20
        ),
        cost_estimate=pl.CostEstimate(
            flops=4 * 30 * cells, bytes_accessed=4 * 8 * cells, transcendentals=0
        ),
    )(
        wp.reshape(cx, ny, nz),
        wn.reshape(cx, ny, nz),
        ax.reshape(cx, ny, nz),
        an.reshape(cx, ny, nz),
        velocity,
        *small,
    )
    out_w, out_a, out_g = pl.pallas_call(
        copy_out,
        out_shape=tuple(jax.ShapeDtypeStruct(shape, f32) for shape in shapes),
        in_specs=[vmem] * 3,
        out_specs=(any_space,) * 3,
        scratch_shapes=[dma((5,))],
        compiler_params=pltpu.CompilerParams(vmem_limit_bytes=2**20),
        cost_estimate=pl.CostEstimate(flops=0, bytes_accessed=8 * 4 * cells, transcendentals=0),
    )(*(pltpu.with_memory_space_constraint(v, pltpu.VMEM) for v in results))
    return out_w[None], out_a[None], out_g


def solution(mesh):
    fields = P("shot", "gx", None, None)
    return jax.shard_map(
        functools.partial(per_device, mesh.shape["gx"], mesh.shape["shot"]),
        mesh=mesh,
        in_specs=(fields,) * 4
        + (P("gx", None, None), P("shot", None, "gx"), P(), P(), P(), P(), P("gx")),
        out_specs=(fields, fields, P("gx", "shot", None)),
        check_vma=False,
    )
```
